32 devices in a mesh: groups: 1, gcol: 16 (over z, y, x), grow: 2 (over core).
Axes of the slice: x: 2, y: 2, z: 4, core: 2. Of those that a mesh axis runs over, the one named last changes fastest.
Arguments:
- ancestor_inverse: bfloat16 [6144, 6144], P(('groups', 'gcol')), may hold values from -6 to 6
- lower_rows: bfloat16 [2, 4096, 1024], P('groups', 'gcol'), may hold values from -0.09375 to 0.09375
- factor_inverse: bfloat16 [2, 1024, 1024], P('groups', 'gcol'), may hold values from -0.1875 to 0.1875
- block_lists: int32 [2, 32], P('groups'), may hold values from 0 to 47, as said below
- live_counts: int32 [2], P('groups'), may hold values from 16 to 32, as said below
Outputs:
- ancestor_columns: bfloat16 [2, 6144, 1024], P('groups', 'gcol', 'grow')
- diagonal_inverse: float32 [2, 2, 512, 1024], P('groups', 'grow', 'gcol')
The draws below stay inside these ranges and needn't reach their ends.
Inputs may be any that keep to these rules, and one draw needn't show every extreme that they name: `live_counts`: supernode 0 uses all 32 slots; the other supernodes use at least half of them. `block_lists`: in each supernode all entries are distinct; the live slots come first in increasing order of pool block.
All inputs are finite; a program needn't handle non-finite values.
Results may differ from the reference program's by a relative error of at most 0.0057.
Values may be sent and summed in bfloat16 or wider, within the bound.
A program may use at most 128 MiB of HBM per device.

```python
import jax
import jax.numpy as jnp
from jax import lax

W = 1024
BLK = 128
S = 2
NS = 32
M = 4096
NB = 48
R = 6144
N_GROW = 2


def shared_counts(key):
    others = jax.random.randint(jax.random.fold_in(key, 11), (S - 1,), NS // 2, NS + 1)
    return jnp.concatenate([jnp.full((1,), NS, jnp.int32), others.astype(jnp.int32)])


def draw_live_counts(key, part):
    counts = shared_counts(key)
    return counts.astype(jnp.int32)


def draw_block_lists(key, part):
    counts = shared_counts(key)
    key = jax.random.fold_in(key, 5)
    listing = []
    for node in range(S):
        chosen = jax.random.permutation(jax.random.fold_in(key, node), NB)[:NS].astype(jnp.int32)
        keyed = jnp.where(jnp.arange(NS, dtype=jnp.int32) < counts[node], chosen, chosen + NB)
        ordered = jnp.sort(keyed)
        listing.append(jnp.where(ordered >= NB, ordered - NB, ordered))
    return jnp.stack(listing).astype(jnp.int32)


def block_levels(rng, dims, shards, low, high):
    def one(dim, blocks):
        heights = jax.random.uniform(jax.random.fold_in(jax.random.fold_in(rng, 6), dim), (blocks,), jnp.float32, low / len(shards), high / len(shards))
        return jnp.repeat(jnp.exp(heights), dims[dim] // blocks).reshape((-1,) + (1,) * (len(dims) - dim - 1))

    level = one(*shards[0])
    for cut in shards[1:]:
        level = level * one(*cut)
    return level


def noise(own_key, dims, scale, bound, split=(), kind=jnp.bfloat16):
    result = jax.random.normal(own_key, dims, jnp.float32) * scale
    if len(split) > 0:
        result = block_levels(own_key, dims, split, -0.22, 0.18) * result
    return jnp.clip(result, min=-bound, max=bound).astype(kind)


def setup_inputs(seed: int = 0, part: int = 0) -> dict:
    key_list = jax.random.split(jax.random.key(seed), 6)
    part_keys = jax.random.split(jax.random.fold_in(key_list[5], part), 6)
    ancestor_inverse = noise(part_keys[0], (R, R), 1.0, 6.0, ((0, 16),))
    lower_rows = noise(part_keys[1], (S, M, W), M ** -0.5, 0.09375, ((1, 16),))
    factor_inverse = noise(part_keys[2], (S, W, W), W ** -0.5, 0.1875, ((1, 16),))
    block_lists = draw_block_lists(jax.random.fold_in(jax.random.fold_in(key_list[5], part), 71), part)
    live_counts = draw_live_counts(jax.random.fold_in(jax.random.fold_in(key_list[5], part), 71), part)
    return dict(ancestor_inverse=ancestor_inverse, lower_rows=lower_rows, factor_inverse=factor_inverse, block_lists=block_lists, live_counts=live_counts)


def reference(ancestor_inverse, lower_rows, factor_inverse, block_lists, live_counts):
    pool = ancestor_inverse.astype(jnp.float32)
    ancestors = []
    diagonals = []
    for node in range(S):
        lower = lower_rows[node].astype(jnp.float32)
        inverse_factor = factor_inverse[node].astype(jnp.float32)
        listing = block_lists[node].astype(jnp.int32)
        live = jnp.arange(NS, dtype=jnp.int32) < live_counts[node]
        row_live = jnp.repeat(live, BLK)
        scaled = jnp.dot(lower, inverse_factor, precision=lax.Precision.HIGHEST)
        scaled = jnp.where(row_live[:, None], scaled, 0.0).astype(jnp.bfloat16)
        columns = (listing[:, None] * BLK + jnp.arange(BLK, dtype=jnp.int32)[None, :]).reshape(-1)
        selected = jnp.take(pool, columns, axis=1)
        product = jnp.dot(selected, scaled.astype(jnp.float32), precision=lax.Precision.HIGHEST)
        matches = (listing[None, :] == jnp.arange(NB, dtype=jnp.int32)[:, None]) & live[None, :]
        member = jnp.any(matches, axis=1)
        slot_of = jnp.sum(jnp.where(matches, jnp.arange(NS, dtype=jnp.int32)[None, :], 0), axis=1).astype(jnp.int32)
        member_rows = jnp.repeat(member, BLK)
        ancestor = jnp.where(member_rows[:, None], -product, 0.0).astype(jnp.bfloat16)
        wanted = (slot_of[:, None] * BLK + jnp.arange(BLK, dtype=jnp.int32)[None, :]).reshape(-1)
        picked = jnp.take(scaled, wanted, axis=0).astype(jnp.float32)
        shared = jnp.dot(picked.T, ancestor.astype(jnp.float32), precision=lax.Precision.HIGHEST)
        own_term = jnp.dot(inverse_factor.T, inverse_factor, precision=lax.Precision.HIGHEST)
        diagonal = own_term - shared
        ancestors.append(ancestor)
        diagonals.append(diagonal.reshape(N_GROW, W // N_GROW, W))
    return jnp.stack(ancestors), jnp.stack(diagonals)
```

```python
import functools

import jax
import jax.numpy as jnp
from jax import lax
from jax.experimental import pallas as pl
from jax.experimental.pallas import tpu as pltpu
from jax.sharding import PartitionSpec as P

BLK = 128
MESH = pl.DeviceIdType.MESH
F32 = jnp.float32
BF16 = jnp.bfloat16


def guarded(pred, action):
    if pred is None:
        action()
    else:
        pl.when(pred)(action)


class Net:
    def __init__(self, send_sems, recv_sems):
        self.send_sems, self.recv_sems = send_sems, recv_sems
        self.used = 0
        self.pending = []

    def take(self, count):
        base = self.used
        self.used += count
        return base

    def push(self, src, dst, send, recv, device, pred=None):
        def copy():
            return pltpu.make_async_remote_copy(
                src_ref=src,
                dst_ref=dst,
                send_sem=self.send_sems.at[send],
                recv_sem=self.recv_sems.at[recv],
                device_id=device,
                device_id_type=MESH,
            )

        guarded(pred, lambda: copy().start())
        self.pending.append((pred, copy))

    def arrived(self, dst, recv, device, pred=None):
        def wait():
            pltpu.make_async_remote_copy(
                src_ref=dst,
                dst_ref=dst,
                send_sem=self.send_sems.at[recv],
                recv_sem=self.recv_sems.at[recv],
                device_id=device,
                device_id_type=MESH,
            ).wait_recv()

        guarded(pred, wait)

    def drain(self):
        for pred, copy in self.pending:
            guarded(pred, lambda copy=copy: copy().wait_send())


def run(tasks):
    active = list(tasks)
    while active:
        for task in list(active):
            try:
                next(task)
            except StopIteration:
                active.remove(task)


def together(tasks):
    active = list(tasks)
    while active:
        for task in list(active):
            try:
                next(task)
            except StopIteration:
                active.remove(task)
        yield


def gather(net, view, order, pos, sizes, peer):
    z, planes = pos["z"], sizes["z"]

    def region(zs, done, flip=None):
        index = {}
        for axis in "yx":
            if axis in done:
                index[axis] = slice(None)
            else:
                index[axis] = 1 - pos[axis] if axis == flip else pos[axis]
        return view(zs, index["y"], index["x"])

    place = order.index("z")
    before = [axis for axis in order[:place] if sizes[axis] > 1]
    after = [axis for axis in order[place + 1 :] if sizes[axis] > 1]
    done = set()
    for axis in before:
        sem = net.take(1)
        mine = region(z, done)
        net.push(mine, mine, sem, sem, peer(axis))
        yield
        net.arrived(region(z, done, axis), sem, peer(axis))
        done = done | {axis}
    bases = {axis: net.take(planes) for axis in after}
    up, down = net.take(planes), net.take(planes)

    def forward(axis, zs, finished, pred):
        piece = region(zs, finished)
        net.push(piece, piece, bases[axis] + zs, bases[axis] + zs, peer(axis), pred)

    for k in range(planes - 1):
        lower, upper = z - k, z + k
        piece = region(lower, done)
        net.push(piece, piece, up + lower, up + lower, peer("z", z + 1), (z < planes - 1) & (lower >= 0))
        piece = region(upper, done)
        net.push(piece, piece, down + upper, down + upper, peer("z", z - 1), (z > 0) & (upper < planes))
        if k == 0 and after:
            forward(after[0], z, done, None)
        yield
        lower, upper = lower - 1, upper + 1
        net.arrived(region(lower, done), up + lower, peer("z", z - 1), lower >= 0)
        if after:
            forward(after[0], lower, done, lower >= 0)
        net.arrived(region(upper, done), down + upper, peer("z", z + 1), upper < planes)
        if after:
            forward(after[0], upper, done, upper < planes)
    for i, axis in enumerate(after):
        for far in range(planes):
            yield
            for zs, pred in [(z, None)] if far == 0 else [(z - far, z >= far), (z + far, z + far < planes)]:
                net.arrived(region(zs, done, axis), bases[axis] + zs, peer(axis), pred)
                if i + 1 < len(after):
                    forward(after[i + 1], zs, done | {axis}, pred)
        done = done | {axis}


def kernel(
    sizes, live_ref, hit_ref, factor_ref, lower_ref, chosen_hbm, anc_ref, diag_ref,
    chosen, fbuf, sbufs, acc, picked_acc, own_neg, other_neg, terms, kept,
    send_a, recv_a, send_b, recv_b, send_c, recv_c, send_sems, recv_sems, chosen_sem,
):
    nz, ny, nx = sizes["z"], sizes["y"], sizes["x"]
    supernodes, piece_rows, order_size = factor_ref.shape
    slot_rows = lower_ref.shape[1]
    slot_dev = slot_rows // BLK
    slot_total = hit_ref.shape[2]
    own_rows = chosen_hbm.shape[1]
    own_blocks = own_rows // BLK
    half = order_size // 2
    out_rows = diag_ref.shape[1]
    column = lax.axis_index("gcol")
    parity = lax.axis_index("grow")
    x = column % nx
    y = (column // nx) % ny
    z = column // (nx * ny)
    pos = {"z": z, "y": y, "x": x}
    own_cols = pl.ds(pl.multiple_of(parity * half, half), half)
    other_cols = pl.ds(pl.multiple_of((1 - parity) * half, half), half)
    mate = {"grow": 1 - parity}

    def peer(axis, to=None):
        if axis == "x":
            return {"gcol": (z * ny + y) * nx + 1 - x}
        if axis == "y":
            return {"gcol": (z * ny + 1 - y) * nx + x}
        return {"gcol": (to * ny + y) * nx + x}

    chosen_copy = pltpu.make_async_copy(chosen_hbm, chosen, chosen_sem)
    chosen_copy.start()
    barrier = pltpu.get_barrier_semaphore()
    greeted = [mate] + [peer(axis) for axis in "xy" if sizes[axis] > 1]
    greeted += [peer("z", (z + d) % nz) for d in range(1, nz)]
    for device in greeted:
        pl.semaphore_signal(barrier, inc=1, device_id=device, device_id_type=MESH)
    for s in range(supernodes):
        fbuf[s, z, y, x] = factor_ref[s, :, own_cols]
    members = [
        [sum(hit_ref[s, b, j] for j in range(slot_total)) for b in range(own_blocks)] for s in range(supernodes)
    ]
    pl.semaphore_wait(barrier, len(greeted))

    net = Net(send_sems, recv_sems)
    orders = ["xzy", "yzx", "zxy", "zyx"] if nx * ny > 1 else ["zxy"]

    def gathers(make_view, rows):
        count = min(len(orders), rows // 16)
        step = rows // count
        return [
            gather(net, make_view(pl.ds(i * step, step)), orders[i], pos, sizes, peer) for i in range(count)
        ]

    run(gathers(lambda rows: lambda zs, ys, xs: fbuf.at[:, zs, ys, xs, rows, :], piece_rows))

    def scale(s):
        whole = fbuf[s].reshape(order_size, half)
        product = jnp.dot(lower_ref[s], whole, preferred_element_type=F32)
        for j in range(slot_dev):
            rows = slice(j * BLK, (j + 1) * BLK)
            sbufs[s][z, y, x, rows, :] = (product[rows] * live_ref[s, j]).astype(BF16)

    def scatter(s, u):
        first, second = ("x", "y") if u == 0 else ("y", "x")
        cols = own_cols if u == 0 else other_cols
        if nx * ny > 1:
            def part(one, two):
                index = {first: one, second: two}
                return terms[s, u, :, index["y"], index["x"]]

            a, b = pos[first], pos[second]
            for other in range(2):
                send_a[s, u, :, other] = part(1 - a, other).astype(BF16)
            sem = net.take(1)
            net.push(send_a.at[s, u], recv_a.at[s, u], sem, sem, peer(first))
            yield
            net.arrived(recv_a.at[s, u], sem, peer(first))
            send_b[s, u] = (part(a, 1 - b) + recv_a[s, u, :, 1 - b].astype(F32)).astype(BF16)
            sem = net.take(1)
            net.push(send_b.at[s, u], recv_b.at[s, u], sem, sem, peer(second))
            kept[s, u] = part(a, b) + recv_a[s, u, :, b].astype(F32)
            yield
            net.arrived(recv_b.at[s, u], sem, peer(second))
            kept[s, u] = kept[s, u] + recv_b[s, u].astype(F32)
        else:
            kept[s, u] = terms[s, u, :, 0, 0]
        send_c[s, u] = kept[s, u].astype(BF16)
        sem = net.take(nz)
        for d in range(1, nz):
            to = (z + d) % nz
            net.push(send_c.at[s, u, to], recv_c.at[s, u, d - 1], sem + d, sem + d, peer("z", to))
        yield
        total = kept[s, u, z]
        for d in range(1, nz):
            net.arrived(recv_c.at[s, u, d - 1], sem + d, peer("z", (z + d) % nz))
            total = total + recv_c[s, u, d - 1].astype(F32)
        diag_ref[s, :, cols] = total

    def finish(s):
        for plane in range(nz):
            width = ny * nx * slot_rows
            part = jnp.dot(
                chosen[s, :, plane * width : (plane + 1) * width],
                sbufs[s][plane].reshape(width, half),
                preferred_element_type=F32,
            )
            if plane == 0:
                acc[s] = part
            elif plane < nz - 1:
                acc[s] = acc[s] + part
            else:
                total = acc[s] + part
            for b in range(own_blocks):
                found = picked_acc[s, b] if plane > 0 else jnp.zeros((BLK, half), BF16)
                for i in range(ny * nx * slot_dev):
                    chip = i // slot_dev
                    rows = slice(i % slot_dev * BLK, (i % slot_dev + 1) * BLK)
                    weight = hit_ref[s, b, plane * ny * nx * slot_dev + i]
                    found += sbufs[s][plane, chip // nx, chip % nx, rows, :] * jnp.full((BLK, half), weight).astype(BF16)
                picked_acc[s, b] = found
            yield
        for b in range(own_blocks):
            rows = slice(b * BLK, (b + 1) * BLK)
            block = (total[rows] * members[s][b]).astype(BF16)
            own_neg[s, rows, :] = block
            anc_ref[s, rows, :] = -block
        sem = net.take(1)
        net.push(own_neg.at[s], other_neg.at[s], sem, sem, mate)
        left = jnp.concatenate([picked_acc[s].reshape(own_rows, half), factor_ref[s, :, own_cols]], axis=0)

        def term(u, neg, cols):
            right = jnp.concatenate([neg[s], factor_ref[s, :, cols]], axis=0)
            result = lax.dot_general(left, right, (((0,), (0,)), ((), ())), preferred_element_type=F32)
            terms[s, u] = result.reshape(nz, ny, nx, out_rows, half)

        term(0, own_neg, own_cols)
        lower_half = scatter(s, 0)
        next(lower_half)
        yield
        net.arrived(other_neg.at[s], sem, mate)
        term(1, other_neg, other_cols)
        yield from together([lower_half, scatter(s, 1)])

    def node(s):
        for _ in range(4 * s):
            yield
        scale(s)
        yield from together(
            gathers(lambda rows: lambda zs, ys, xs: sbufs[s].at[zs, ys, xs, rows, :], slot_rows)
        )
        if s == 0:
            chosen_copy.wait()
        yield from finish(s)

    run([node(s) for s in range(supernodes)])
    net.drain()


def choose(slot_dev, live_ref, list_ref, pool_hbm, chosen_hbm, live_out, hit_out, sems):
    column = lax.axis_index("gcol")
    supernodes, own_blocks, slot_total = hit_out.shape
    copies = []
    for s in range(supernodes):
        for j in range(slot_total):
            block = list_ref[s, j]
            copy = pltpu.make_async_copy(
                pool_hbm.at[:, pl.ds(pl.multiple_of(block * BLK, BLK), BLK)],
                chosen_hbm.at[s, :, pl.ds(j * BLK, BLK)],
                sems.at[s, j],
            )
            copy.start()
            copies.append(copy)
    for s in range(supernodes):
        live = live_ref[s]
        for j in range(slot_dev):
            live_out[s, j] = jnp.where(column * slot_dev + j < live, 1.0, 0.0)
        for j in range(slot_total):
            for b in range(own_blocks):
                match = (list_ref[s, j] == column * own_blocks + b) & (j < live)
                hit_out[s, b, j] = jnp.where(match, 1.0, 0.0)
    for copy in copies:
        copy.wait()


def shards(ancestor_inverse, lower_rows, factor_inverse, block_lists, live_counts):
    supernodes, slot_rows, order_size = lower_rows.shape
    own_rows = ancestor_inverse.shape[0]
    piece_rows = factor_inverse.shape[1]
    columns = lax.axis_size("gcol")
    side = 2 if lax.axis_size("groups") == 1 and columns % 4 == 0 else 1
    nz = columns // (side * side)
    sizes = {"z": nz, "y": side, "x": side}
    half = order_size // lax.axis_size("grow")
    out_rows = half // columns
    grid = (nz, side, side)
    sems = (1 + supernodes) * (4 if side > 1 else 1) * (4 * nz + 2) + supernodes * (1 + 2 * (2 + nz))
    slot_total = block_lists.shape[1]
    slot_dev = slot_rows // BLK
    chosen_shape = (supernodes, own_rows, slot_total * BLK)
    smem = pl.BlockSpec(memory_space=pltpu.SMEM)
    chosen, live, hit = pl.pallas_call(
        functools.partial(choose, slot_dev),
        out_shape=(
            jax.ShapeDtypeStruct(chosen_shape, BF16),
            jax.ShapeDtypeStruct((supernodes, slot_dev), F32),
            jax.ShapeDtypeStruct((supernodes, own_rows // BLK, slot_total), F32),
        ),
        in_specs=[smem, smem, pl.BlockSpec(memory_space=pl.ANY)],
        out_specs=(pl.BlockSpec(memory_space=pl.ANY), smem, smem),
        scratch_shapes=[pltpu.SemaphoreType.DMA((supernodes, slot_total))],
    )(live_counts, block_lists, ancestor_inverse)
    ancestor, diagonal = pl.pallas_call(
        functools.partial(kernel, sizes),
        out_shape=(
            jax.ShapeDtypeStruct((supernodes, own_rows, half), BF16),
            jax.ShapeDtypeStruct((supernodes, out_rows, order_size), F32),
        ),
        in_specs=[
            pl.BlockSpec(memory_space=pltpu.SMEM),
            pl.BlockSpec(memory_space=pltpu.SMEM),
            pl.BlockSpec(memory_space=pltpu.VMEM),
            pl.BlockSpec(memory_space=pltpu.VMEM),
            pl.BlockSpec(memory_space=pl.ANY),
        ],
        out_specs=(pl.BlockSpec(memory_space=pltpu.VMEM), pl.BlockSpec(memory_space=pltpu.VMEM)),
        scratch_shapes=[
            pltpu.VMEM(chosen_shape, BF16),
            pltpu.VMEM((supernodes,) + grid + (piece_rows, half), BF16),
            [pltpu.VMEM(grid + (slot_rows, half), BF16) for _ in range(supernodes)],
            pltpu.VMEM((supernodes, own_rows, half), F32),
            pltpu.VMEM((supernodes, own_rows // BLK, BLK, half), BF16),
            pltpu.VMEM((supernodes, own_rows, half), BF16),
            pltpu.VMEM((supernodes, own_rows, half), BF16),
            pltpu.VMEM((supernodes, 2) + grid + (out_rows, half), F32),
            pltpu.VMEM((supernodes, 2, nz, out_rows, half), F32),
            pltpu.VMEM((supernodes, 2, nz, side, out_rows, half), BF16),
            pltpu.VMEM((supernodes, 2, nz, side, out_rows, half), BF16),
            pltpu.VMEM((supernodes, 2, nz, out_rows, half), BF16),
            pltpu.VMEM((supernodes, 2, nz, out_rows, half), BF16),
            pltpu.VMEM((supernodes, 2, nz, out_rows, half), BF16),
            pltpu.VMEM((supernodes, 2, nz, out_rows, half), BF16),
            pltpu.SemaphoreType.DMA((sems,)),
            pltpu.SemaphoreType.DMA((sems,)),
            pltpu.SemaphoreType.DMA,
        ],
        compiler_params=pltpu.CompilerParams(
            collective_id=0, has_side_effects=True, vmem_limit_bytes=58 * 1024 * 1024
        ),
    )(live, hit, factor_inverse, lower_rows, chosen)
    return (ancestor, diagonal[:, None, :, :])


def solution(mesh):
    return jax.shard_map(
        shards,
        mesh=mesh,
        in_specs=(
            P(("groups", "gcol"), None),
            P("groups", "gcol", None),
            P("groups", "gcol", None),
            P("groups", None),
            P("groups"),
        ),
        out_specs=(P("groups", "gcol", "grow"), P("groups", "grow", "gcol", None)),
        check_vma=False,
    )
```

```python
import functools

import jax
import jax.numpy as jnp
from jax import lax
from jax.experimental import pallas as pl
from jax.experimental.pallas import tpu as pltpu
from jax.sharding import PartitionSpec as P

BLK = 128
LAG = 8
PAUSE = 2
MESH = pl.DeviceIdType.MESH
F32 = jnp.float32
BF16 = jnp.bfloat16


def guarded(pred, action):
    if pred is None:
        action()
    else:
        pl.when(pred)(action)


class Net:
    def __init__(self, send_sems, recv_sems):
        self.send_sems, self.recv_sems = send_sems, recv_sems
        self.used = 0
        self.pending = []

    def take(self, count):
        base = self.used
        self.used += count
        return base

    def push(self, src, dst, send, recv, device, pred=None):
        def copy():
            return pltpu.make_async_remote_copy(
                src_ref=src,
                dst_ref=dst,
                send_sem=self.send_sems.at[send],
                recv_sem=self.recv_sems.at[recv],
                device_id=device,
                device_id_type=MESH,
            )

        guarded(pred, lambda: copy().start())
        self.pending.append((pred, copy))

    def arrived(self, dst, recv, device, pred=None):
        def wait():
            pltpu.make_async_remote_copy(
                src_ref=dst,
                dst_ref=dst,
                send_sem=self.send_sems.at[recv],
                recv_sem=self.recv_sems.at[recv],
                device_id=device,
                device_id_type=MESH,
            ).wait_recv()

        guarded(pred, wait)

    def drain(self):
        for pred, copy in self.pending:
            guarded(pred, lambda copy=copy: copy().wait_send())


def run(tasks):
    active = list(tasks)
    while active:
        for task in list(active):
            try:
                next(task)
            except StopIteration:
                active.remove(task)


def together(tasks):
    active = list(tasks)
    while active:
        for task in list(active):
            try:
                next(task)
            except StopIteration:
                active.remove(task)
        yield


def gather(net, view, order, pos, sizes, peer):
    z, planes = pos["z"], sizes["z"]

    def region(zs, done, flip=None):
        index = {}
        for axis in "yx":
            if axis in done:
                index[axis] = slice(None)
            else:
                index[axis] = 1 - pos[axis] if axis == flip else pos[axis]
        return view(zs, index["y"], index["x"])

    place = order.index("z")
    before = [axis for axis in order[:place] if sizes[axis] > 1]
    after = [axis for axis in order[place + 1 :] if sizes[axis] > 1]
    done = set()
    for axis in before:
        sem = net.take(1)
        mine = region(z, done)
        net.push(mine, mine, sem, sem, peer(axis))
        yield
        net.arrived(region(z, done, axis), sem, peer(axis))
        done = done | {axis}
    bases = {axis: net.take(planes) for axis in after}
    up, down = net.take(planes), net.take(planes)

    def forward(axis, zs, finished, pred):
        piece = region(zs, finished)
        net.push(piece, piece, bases[axis] + zs, bases[axis] + zs, peer(axis), pred)

    for k in range(planes - 1):
        lower, upper = z - k, z + k
        piece = region(lower, done)
        net.push(piece, piece, up + lower, up + lower, peer("z", z + 1), (z < planes - 1) & (lower >= 0))
        piece = region(upper, done)
        net.push(piece, piece, down + upper, down + upper, peer("z", z - 1), (z > 0) & (upper < planes))
        if k == 0 and after:
            forward(after[0], z, done, None)
        yield
        lower, upper = lower - 1, upper + 1
        net.arrived(region(lower, done), up + lower, peer("z", z - 1), lower >= 0)
        if after:
            forward(after[0], lower, done, lower >= 0)
        net.arrived(region(upper, done), down + upper, peer("z", z + 1), upper < planes)
        if after:
            forward(after[0], upper, done, upper < planes)
    for i, axis in enumerate(after):
        for far in range(planes):
            yield
            for zs, pred in [(z, None)] if far == 0 else [(z - far, z >= far), (z + far, z + far < planes)]:
                net.arrived(region(zs, done, axis), bases[axis] + zs, peer(axis), pred)
                if i + 1 < len(after):
                    forward(after[i + 1], zs, done | {axis}, pred)
        done = done | {axis}


def kernel(
    sizes, live_ref, hit_ref, factor_ref, lower_ref, chosen_hbm, anc_ref, diag_ref,
    chosen, fbuf, sbufs, acc, picked_acc, own_neg, other_neg, terms, kept,
    send_a, recv_a, send_b, recv_b, send_c, recv_c, send_sems, recv_sems, chosen_sem,
):
    nz, ny, nx = sizes["z"], sizes["y"], sizes["x"]
    supernodes, piece_rows, order_size = factor_ref.shape
    slot_rows = lower_ref.shape[1]
    slot_dev = slot_rows // BLK
    slot_total = hit_ref.shape[2]
    own_rows = chosen_hbm.shape[1]
    own_blocks = own_rows // BLK
    half = order_size // 2
    out_rows = diag_ref.shape[1]
    column = lax.axis_index("gcol")
    parity = lax.axis_index("grow")
    x = column % nx
    y = (column // nx) % ny
    z = column // (nx * ny)
    pos = {"z": z, "y": y, "x": x}
    own_cols = pl.ds(pl.multiple_of(parity * half, half), half)
    other_cols = pl.ds(pl.multiple_of((1 - parity) * half, half), half)
    mate = {"grow": 1 - parity}

    def peer(axis, to=None):
        if axis == "x":
            return {"gcol": (z * ny + y) * nx + 1 - x}
        if axis == "y":
            return {"gcol": (z * ny + 1 - y) * nx + x}
        return {"gcol": (to * ny + y) * nx + x}

    chosen_copy = pltpu.make_async_copy(chosen_hbm, chosen, chosen_sem)
    chosen_copy.start()
    barrier = pltpu.get_barrier_semaphore()
    greeted = [mate] + [peer(axis) for axis in "xy" if sizes[axis] > 1]
    greeted += [peer("z", (z + d) % nz) for d in range(1, nz)]
    for device in greeted:
        pl.semaphore_signal(barrier, inc=1, device_id=device, device_id_type=MESH)
    for s in range(supernodes):
        fbuf[s, z, y, x] = factor_ref[s, :, own_cols]
    members = [
        [sum(hit_ref[s, b, j] for j in range(slot_total)) for b in range(own_blocks)] for s in range(supernodes)
    ]
    pl.semaphore_wait(barrier, len(greeted))

    net = Net(send_sems, recv_sems)
    orders = ["xzy", "yzx", "zxy", "zyx"] if nx * ny > 1 else ["zxy"]

    def gathers(make_view, rows, flip=0):
        unit = rows // 16
        shares = [unit // 4] * 4
        if unit == 16:
            shares = [6, 5, 3, 2] if flip == 0 else [5, 6, 2, 3]
        shares = shares[: len(orders)] if len(orders) > 1 else [unit]
        tasks, start = [], 0
        for order, share in zip(orders, shares):
            tasks.append(gather(net, make_view(pl.ds(start, share * 16)), order, pos, sizes, peer))
            start += share * 16
        return tasks

    run(gathers(lambda rows: lambda zs, ys, xs: fbuf.at[:, zs, ys, xs, rows, :], piece_rows))

    def scale(s):
        whole = fbuf[s].reshape(order_size, half)
        product = jnp.dot(lower_ref[s], whole, preferred_element_type=F32)
        for j in range(slot_dev):
            rows = slice(j * BLK, (j + 1) * BLK)
            sbufs[s][z, y, x, rows, :] = (product[rows] * live_ref[s, j]).astype(BF16)

    def scatter(s, u):
        first, second = ("x", "y") if u == 0 else ("y", "x")
        cols = own_cols if u == 0 else other_cols
        if nx * ny > 1:
            def part(one, two):
                index = {first: one, second: two}
                return terms[s, u, :, index["y"], index["x"]]

            a, b = pos[first], pos[second]
            for other in range(2):
                send_a[s, u, :, other] = part(1 - a, other).astype(BF16)
            sem = net.take(1)
            net.push(send_a.at[s, u], recv_a.at[s, u], sem, sem, peer(first))
            for _ in range(PAUSE if s == 0 else 1):
                yield
            net.arrived(recv_a.at[s, u], sem, peer(first))
            send_b[s, u] = (part(a, 1 - b) + recv_a[s, u, :, 1 - b].astype(F32)).astype(BF16)
            sem = net.take(1)
            net.push(send_b.at[s, u], recv_b.at[s, u], sem, sem, peer(second))
            kept[s, u] = part(a, b) + recv_a[s, u, :, b].astype(F32)
            for _ in range(PAUSE if s == 0 else 1):
                yield
            net.arrived(recv_b.at[s, u], sem, peer(second))
            kept[s, u] = kept[s, u] + recv_b[s, u].astype(F32)
        else:
            kept[s, u] = terms[s, u, :, 0, 0]
        send_c[s, u] = kept[s, u].astype(BF16)
        sem = net.take(nz)
        for d in range(1, nz):
            to = (z + d) % nz
            net.push(send_c.at[s, u, to], recv_c.at[s, u, d - 1], sem + d, sem + d, peer("z", to))
        for _ in range(PAUSE if s == 0 else 1):
            yield
        total = kept[s, u, z]
        for d in range(1, nz):
            net.arrived(recv_c.at[s, u, d - 1], sem + d, peer("z", (z + d) % nz))
            total = total + recv_c[s, u, d - 1].astype(F32)
        diag_ref[s, :, cols] = total

    def finish(s):
        for plane in range(nz):
            width = ny * nx * slot_rows
            part = jnp.dot(
                chosen[s, :, plane * width : (plane + 1) * width],
                sbufs[s][plane].reshape(width, half),
                preferred_element_type=F32,
            )
            if plane == 0:
                acc[s] = part
            elif plane < nz - 1:
                acc[s] = acc[s] + part
            else:
                total = acc[s] + part
            for b in range(own_blocks):
                found = picked_acc[s, b] if plane > 0 else jnp.zeros((BLK, half), BF16)
                for i in range(ny * nx * slot_dev):
                    chip = i // slot_dev
                    rows = slice(i % slot_dev * BLK, (i % slot_dev + 1) * BLK)
                    weight = hit_ref[s, b, plane * ny * nx * slot_dev + i]
                    found += sbufs[s][plane, chip // nx, chip % nx, rows, :] * jnp.full((BLK, half), weight).astype(BF16)
                picked_acc[s, b] = found
            yield
        for b in range(own_blocks):
            rows = slice(b * BLK, (b + 1) * BLK)
            block = (total[rows] * members[s][b]).astype(BF16)
            own_neg[s, rows, :] = block
            anc_ref[s, rows, :] = -block
        sem = net.take(1)
        net.push(own_neg.at[s], other_neg.at[s], sem, sem, mate)
        left = jnp.concatenate([picked_acc[s].reshape(own_rows, half), factor_ref[s, :, own_cols]], axis=0)

        def term(u, neg, cols):
            right = jnp.concatenate([neg[s], factor_ref[s, :, cols]], axis=0)
            result = lax.dot_general(left, right, (((0,), (0,)), ((), ())), preferred_element_type=F32)
            terms[s, u] = result.reshape(nz, ny, nx, out_rows, half)

        term(0, own_neg, own_cols)
        lower_half = scatter(s, 0)
        next(lower_half)
        yield
        net.arrived(other_neg.at[s], sem, mate)
        term(1, other_neg, other_cols)
        yield from together([lower_half, scatter(s, 1)])

    def node(s):
        for _ in range(LAG * s):
            yield
        scale(s)
        yield from together(
            gathers(lambda rows: lambda zs, ys, xs: sbufs[s].at[zs, ys, xs, rows, :], slot_rows, s)
        )
        if s == 0:
            chosen_copy.wait()
        yield from finish(s)

    run([node(s) for s in range(supernodes)])
    net.drain()


def choose(slot_dev, live_ref, list_ref, pool_ref, chosen_ref, live_out, hit_out):
    column = lax.axis_index("gcol")
    supernodes, own_blocks, slot_total = hit_out.shape
    for s in range(supernodes):
        for j in range(slot_total):
            start = pl.multiple_of(list_ref[s, j] * BLK, BLK)
            chosen_ref[s, :, j * BLK : (j + 1) * BLK] = pool_ref[:, pl.ds(start, BLK)]

    @pl.when(pl.program_id(0) == 0)
    def _():
        for s in range(supernodes):
            live = live_ref[s]
            for j in range(slot_dev):
                live_out[s, j] = jnp.where(column * slot_dev + j < live, 1.0, 0.0)
            for j in range(slot_total):
                for b in range(own_blocks):
                    match = (list_ref[s, j] == column * own_blocks + b) & (j < live)
                    hit_out[s, b, j] = jnp.where(match, 1.0, 0.0)


def shards(ancestor_inverse, lower_rows, factor_inverse, block_lists, live_counts):
    supernodes, slot_rows, order_size = lower_rows.shape
    own_rows, pool_width = ancestor_inverse.shape
    step_rows = BLK // 2
    piece_rows = factor_inverse.shape[1]
    columns = lax.axis_size("gcol")
    side = 2 if lax.axis_size("groups") == 1 and columns % 4 == 0 else 1
    nz = columns // (side * side)
    sizes = {"z": nz, "y": side, "x": side}
    half = order_size // lax.axis_size("grow")
    out_rows = half // columns
    grid = (nz, side, side)
    sems = (1 + supernodes) * (4 if side > 1 else 1) * (4 * nz + 2) + supernodes * (1 + 2 * (2 + nz))
    slot_total = block_lists.shape[1]
    slot_dev = slot_rows // BLK
    chosen_shape = (supernodes, own_rows, slot_total * BLK)
    smem = pl.BlockSpec(memory_space=pltpu.SMEM)
    chosen, live, hit = pl.pallas_call(
        functools.partial(choose, slot_dev),
        out_shape=(
            jax.ShapeDtypeStruct(chosen_shape, BF16),
            jax.ShapeDtypeStruct((supernodes, slot_dev), F32),
            jax.ShapeDtypeStruct((supernodes, own_rows // BLK, slot_total), F32),
        ),
        grid=(own_rows // step_rows,),
        in_specs=[smem, smem, pl.BlockSpec((step_rows, pool_width), lambda i: (i, 0))],
        out_specs=(
            pl.BlockSpec((supernodes, step_rows, slot_total * BLK), lambda i: (0, i, 0)),
            smem,
            smem,
        ),
        compiler_params=pltpu.CompilerParams(vmem_limit_bytes=58 * 1024 * 1024),
    )(live_counts, block_lists, ancestor_inverse)
    ancestor, diagonal = pl.pallas_call(
        functools.partial(kernel, sizes),
        out_shape=(
            jax.ShapeDtypeStruct((supernodes, own_rows, half), BF16),
            jax.ShapeDtypeStruct((supernodes, out_rows, order_size), F32),
        ),
        in_specs=[
            pl.BlockSpec(memory_space=pltpu.SMEM),
            pl.BlockSpec(memory_space=pltpu.SMEM),
            pl.BlockSpec(memory_space=pltpu.VMEM),
            pl.BlockSpec(memory_space=pltpu.VMEM),
            pl.BlockSpec(memory_space=pl.ANY),
        ],
        out_specs=(pl.BlockSpec(memory_space=pltpu.VMEM), pl.BlockSpec(memory_space=pltpu.VMEM)),
        scratch_shapes=[
            pltpu.VMEM(chosen_shape, BF16),
            pltpu.VMEM((supernodes,) + grid + (piece_rows, half), BF16),
            [pltpu.VMEM(grid + (slot_rows, half), BF16) for _ in range(supernodes)],
            pltpu.VMEM((supernodes, own_rows, half), F32),
            pltpu.VMEM((supernodes, own_rows // BLK, BLK, half), BF16),
            pltpu.VMEM((supernodes, own_rows, half), BF16),
            pltpu.VMEM((supernodes, own_rows, half), BF16),
            pltpu.VMEM((supernodes, 2) + grid + (out_rows, half), F32),
            pltpu.VMEM((supernodes, 2, nz, out_rows, half), F32),
            pltpu.VMEM((supernodes, 2, nz, side, out_rows, half), BF16),
            pltpu.VMEM((supernodes, 2, nz, side, out_rows, half), BF16),
            pltpu.VMEM((supernodes, 2, nz, out_rows, half), BF16),
            pltpu.VMEM((supernodes, 2, nz, out_rows, half), BF16),
            pltpu.VMEM((supernodes, 2, nz, out_rows, half), BF16),
            pltpu.VMEM((supernodes, 2, nz, out_rows, half), BF16),
            pltpu.SemaphoreType.DMA((sems,)),
            pltpu.SemaphoreType.DMA((sems,)),
            pltpu.SemaphoreType.DMA,
        ],
        compiler_params=pltpu.CompilerParams(
            collective_id=0, has_side_effects=True, vmem_limit_bytes=58 * 1024 * 1024
        ),
    )(live, hit, factor_inverse, lower_rows, chosen)
    return (ancestor, diagonal[:, None, :, :])


def solution(mesh):
    return jax.shard_map(
        shards,
        mesh=mesh,
        in_specs=(
            P(("groups", "gcol"), None),
            P("groups", "gcol", None),
            P("groups", "gcol", None),
            P("groups", None),
            P("groups"),
        ),
        out_specs=(P("groups", "gcol", "grow"), P("groups", "grow", "gcol", None)),
        check_vma=False,
    )
```

```python
import functools

import jax
import jax.numpy as jnp
from jax import lax
from jax.experimental import pallas as pl
from jax.experimental.pallas import tpu as pltpu
from jax.sharding import PartitionSpec as P

BLK = 128
LAG = 8
CHUNKS = 2
PAUSE = 3
MESH = pl.DeviceIdType.MESH
F32 = jnp.float32
BF16 = jnp.bfloat16


def guarded(pred, action):
    if pred is None:
        action()
    else:
        pl.when(pred)(action)


class Net:
    def __init__(self, send_sems, recv_sems):
        self.send_sems, self.recv_sems = send_sems, recv_sems
        self.used = 0
        self.pending = []

    def take(self, count):
        base = self.used
        self.used += count
        return base

    def push(self, src, dst, send, recv, device, pred=None):
        def copy():
            return pltpu.make_async_remote_copy(
                src_ref=src,
                dst_ref=dst,
                send_sem=self.send_sems.at[send],
                recv_sem=self.recv_sems.at[recv],
                device_id=device,
                device_id_type=MESH,
            )

        guarded(pred, lambda: copy().start())
        self.pending.append((pred, copy))

    def arrived(self, dst, recv, device, pred=None):
        def wait():
            pltpu.make_async_remote_copy(
                src_ref=dst,
                dst_ref=dst,
                send_sem=self.send_sems.at[recv],
                recv_sem=self.recv_sems.at[recv],
                device_id=device,
                device_id_type=MESH,
            ).wait_recv()

        guarded(pred, wait)

    def drain(self):
        for pred, copy in self.pending:
            guarded(pred, lambda copy=copy: copy().wait_send())


def run(tasks):
    active = list(tasks)
    while active:
        for task in list(active):
            try:
                next(task)
            except StopIteration:
                active.remove(task)


def together(tasks):
    active = list(tasks)
    while active:
        for task in list(active):
            try:
                next(task)
            except StopIteration:
                active.remove(task)
        yield


def gather(net, view, order, pos, sizes, peer):
    z, planes = pos["z"], sizes["z"]

    def region(zs, done, flip=None):
        index = {}
        for axis in "yx":
            if axis in done:
                index[axis] = slice(None)
            else:
                index[axis] = 1 - pos[axis] if axis == flip else pos[axis]
        return view(zs, index["y"], index["x"])

    place = order.index("z")
    before = [axis for axis in order[:place] if sizes[axis] > 1]
    after = [axis for axis in order[place + 1 :] if sizes[axis] > 1]
    done = set()
    for axis in before:
        sem = net.take(1)
        mine = region(z, done)
        net.push(mine, mine, sem, sem, peer(axis))
        yield
        net.arrived(region(z, done, axis), sem, peer(axis))
        done = done | {axis}
    bases = {axis: net.take(planes) for axis in after}
    up, down = net.take(planes), net.take(planes)

    def forward(axis, zs, finished, pred):
        piece = region(zs, finished)
        net.push(piece, piece, bases[axis] + zs, bases[axis] + zs, peer(axis), pred)

    for k in range(planes - 1):
        lower, upper = z - k, z + k
        piece = region(lower, done)
        net.push(piece, piece, up + lower, up + lower, peer("z", z + 1), (z < planes - 1) & (lower >= 0))
        piece = region(upper, done)
        net.push(piece, piece, down + upper, down + upper, peer("z", z - 1), (z > 0) & (upper < planes))
        if k == 0 and after:
            forward(after[0], z, done, None)
        yield
        lower, upper = lower - 1, upper + 1
        net.arrived(region(lower, done), up + lower, peer("z", z - 1), lower >= 0)
        if after:
            forward(after[0], lower, done, lower >= 0)
        net.arrived(region(upper, done), down + upper, peer("z", z + 1), upper < planes)
        if after:
            forward(after[0], upper, done, upper < planes)
    for i, axis in enumerate(after):
        for far in range(planes):
            yield
            for zs, pred in [(z, None)] if far == 0 else [(z - far, z >= far), (z + far, z + far < planes)]:
                net.arrived(region(zs, done, axis), bases[axis] + zs, peer(axis), pred)
                if i + 1 < len(after):
                    forward(after[i + 1], zs, done | {axis}, pred)
        done = done | {axis}


def kernel(
    sizes, live_ref, hit_ref, factor_ref, lower_ref, chosen_hbm, anc_ref, diag_ref,
    chosen, fbuf, sbufs, acc, picked_acc, own_neg, other_neg, terms, kept,
    send_a, recv_a, send_b, recv_b, send_c, recv_c, send_sems, recv_sems, chosen_sem,
):
    nz, ny, nx = sizes["z"], sizes["y"], sizes["x"]
    supernodes, piece_rows, order_size = factor_ref.shape
    slot_rows = lower_ref.shape[1]
    slot_dev = slot_rows // BLK
    slot_total = hit_ref.shape[2]
    own_rows = chosen_hbm.shape[1]
    own_blocks = own_rows // BLK
    half = order_size // 2
    out_rows = diag_ref.shape[1]
    column = lax.axis_index("gcol")
    parity = lax.axis_index("grow")
    x = column % nx
    y = (column // nx) % ny
    z = column // (nx * ny)
    pos = {"z": z, "y": y, "x": x}
    own_cols = pl.ds(pl.multiple_of(parity * half, half), half)
    other_cols = pl.ds(pl.multiple_of((1 - parity) * half, half), half)
    mate = {"grow": 1 - parity}

    def peer(axis, to=None):
        if axis == "x":
            return {"gcol": (z * ny + y) * nx + 1 - x}
        if axis == "y":
            return {"gcol": (z * ny + 1 - y) * nx + x}
        return {"gcol": (to * ny + y) * nx + x}

    chosen_copy = pltpu.make_async_copy(chosen_hbm, chosen, chosen_sem)
    chosen_copy.start()
    barrier = pltpu.get_barrier_semaphore()
    greeted = [mate] + [peer(axis) for axis in "xy" if sizes[axis] > 1]
    greeted += [peer("z", (z + d) % nz) for d in range(1, nz)]
    for device in greeted:
        pl.semaphore_signal(barrier, inc=1, device_id=device, device_id_type=MESH)
    for s in range(supernodes):
        fbuf[s, z, y, x] = factor_ref[s, :, own_cols]
    members = [
        [sum(hit_ref[s, b, j] for j in range(slot_total)) for b in range(own_blocks)] for s in range(supernodes)
    ]
    pl.semaphore_wait(barrier, len(greeted))

    net = Net(send_sems, recv_sems)
    orders = ["xzy", "yzx", "zxy", "zyx"] if nx * ny > 1 else ["zxy"]

    def gathers(make_view, rows, flip=0):
        unit = rows // 16
        shares = [unit // 4] * 4
        if unit == 16:
            shares = [6, 5, 3, 2] if flip == 0 else [5, 6, 2, 3]
        shares = shares[: len(orders)] if len(orders) > 1 else [unit]
        tasks, start = [], 0
        for order, share in zip(orders, shares):
            tasks.append(gather(net, make_view(pl.ds(start, share * 16)), order, pos, sizes, peer))
            start += share * 16
        return tasks

    run(gathers(lambda rows: lambda zs, ys, xs: fbuf.at[:, zs, ys, xs, rows, :], piece_rows))

    def scale(s):
        whole = fbuf[s].reshape(order_size, half)
        product = jnp.dot(lower_ref[s], whole, preferred_element_type=F32)
        for j in range(slot_dev):
            rows = slice(j * BLK, (j + 1) * BLK)
            sbufs[s][z, y, x, rows, :] = (product[rows] * live_ref[s, j]).astype(BF16)

    def scatter(s, u, h):
        width = half // CHUNKS
        span = pl.ds(h * width, width)
        first, second = ("x", "y") if u == 0 else ("y", "x")
        side = parity if u == 0 else 1 - parity
        cols = pl.ds(pl.multiple_of(side * half + h * width, width), width)
        if nx * ny > 1:
            def part(one, two):
                index = {first: one, second: two}
                return terms[s, u, :, index["y"], index["x"], :, span]

            a, b = pos[first], pos[second]
            for other in range(2):
                send_a[s, u, h, :, other] = part(1 - a, other).astype(BF16)
            sem = net.take(1)
            net.push(send_a.at[s, u, h], recv_a.at[s, u, h], sem, sem, peer(first))
            for _ in range(PAUSE if s == 0 else 1):
                yield
            net.arrived(recv_a.at[s, u, h], sem, peer(first))
            send_b[s, u, h] = (part(a, 1 - b) + recv_a[s, u, h, :, 1 - b].astype(F32)).astype(BF16)
            sem = net.take(1)
            net.push(send_b.at[s, u, h], recv_b.at[s, u, h], sem, sem, peer(second))
            kept[s, u, h] = part(a, b) + recv_a[s, u, h, :, b].astype(F32)
            for _ in range(PAUSE if s == 0 else 1):
                yield
            net.arrived(recv_b.at[s, u, h], sem, peer(second))
            kept[s, u, h] = kept[s, u, h] + recv_b[s, u, h].astype(F32)
        else:
            kept[s, u, h] = terms[s, u, :, 0, 0, :, span]
        send_c[s, u, h] = kept[s, u, h].astype(BF16)
        sem = net.take(nz)
        for d in range(1, nz):
            to = (z + d) % nz
            net.push(send_c.at[s, u, h, to], recv_c.at[s, u, h, d - 1], sem + d, sem + d, peer("z", to))
        for _ in range(PAUSE if s == 0 else 1):
            yield
        total = kept[s, u, h, z]
        for d in range(1, nz):
            net.arrived(recv_c.at[s, u, h, d - 1], sem + d, peer("z", (z + d) % nz))
            total = total + recv_c[s, u, h, d - 1].astype(F32)
        diag_ref[s, :, cols] = total

    def finish(s):
        for plane in range(nz):
            width = ny * nx * slot_rows
            part = jnp.dot(
                chosen[s, :, plane * width : (plane + 1) * width],
                sbufs[s][plane].reshape(width, half),
                preferred_element_type=F32,
            )
            if plane == 0:
                acc[s] = part
            elif plane < nz - 1:
                acc[s] = acc[s] + part
            else:
                total = acc[s] + part
            for b in range(own_blocks):
                found = picked_acc[s, b] if plane > 0 else jnp.zeros((BLK, half), BF16)
                for i in range(ny * nx * slot_dev):
                    chip = i // slot_dev
                    rows = slice(i % slot_dev * BLK, (i % slot_dev + 1) * BLK)
                    weight = hit_ref[s, b, plane * ny * nx * slot_dev + i]
                    found += sbufs[s][plane, chip // nx, chip % nx, rows, :] * jnp.full((BLK, half), weight).astype(BF16)
                picked_acc[s, b] = found
            yield
        for b in range(own_blocks):
            rows = slice(b * BLK, (b + 1) * BLK)
            block = (total[rows] * members[s][b]).astype(BF16)
            own_neg[s, rows, :] = block
            anc_ref[s, rows, :] = -block
        sem = net.take(1)
        net.push(own_neg.at[s], other_neg.at[s], sem, sem, mate)
        left = jnp.concatenate([picked_acc[s].reshape(own_rows, half), factor_ref[s, :, own_cols]], axis=0)

        def term(u, neg, cols):
            right = jnp.concatenate([neg[s], factor_ref[s, :, cols]], axis=0)
            result = lax.dot_general(left, right, (((0,), (0,)), ((), ())), preferred_element_type=F32)
            terms[s, u] = result.reshape(nz, ny, nx, out_rows, half)

        term(0, own_neg, own_cols)
        lower = [scatter(s, 0, h) for h in range(CHUNKS)]
        for task in lower:
            next(task)
        yield
        net.arrived(other_neg.at[s], sem, mate)
        term(1, other_neg, other_cols)
        upper = [scatter(s, 1, h) for h in range(CHUNKS)]
        yield from together([task for pair in zip(lower, upper) for task in pair])

    def node(s):
        for _ in range(LAG * s):
            yield
        scale(s)
        yield from together(
            gathers(lambda rows: lambda zs, ys, xs: sbufs[s].at[zs, ys, xs, rows, :], slot_rows, s)
        )
        if s == 0:
            chosen_copy.wait()
        yield from finish(s)

    run([node(s) for s in range(supernodes)])
    net.drain()


def choose(slot_dev, live_ref, list_ref, pool_ref, chosen_ref, live_out, hit_out):
    column = lax.axis_index("gcol")
    supernodes, own_blocks, slot_total = hit_out.shape
    for s in range(supernodes):
        for j in range(slot_total):
            start = pl.multiple_of(list_ref[s, j] * BLK, BLK)
            chosen_ref[s, :, j * BLK : (j + 1) * BLK] = pool_ref[:, pl.ds(start, BLK)]

    @pl.when(pl.program_id(0) == 0)
    def _():
        for s in range(supernodes):
            live = live_ref[s]
            for j in range(slot_dev):
                live_out[s, j] = jnp.where(column * slot_dev + j < live, 1.0, 0.0)
            for j in range(slot_total):
                for b in range(own_blocks):
                    match = (list_ref[s, j] == column * own_blocks + b) & (j < live)
                    hit_out[s, b, j] = jnp.where(match, 1.0, 0.0)


def shards(ancestor_inverse, lower_rows, factor_inverse, block_lists, live_counts):
    supernodes, slot_rows, order_size = lower_rows.shape
    own_rows, pool_width = ancestor_inverse.shape
    step_rows = BLK
    piece_rows = factor_inverse.shape[1]
    columns = lax.axis_size("gcol")
    side = 2 if lax.axis_size("groups") == 1 and columns % 4 == 0 else 1
    nz = columns // (side * side)
    sizes = {"z": nz, "y": side, "x": side}
    half = order_size // lax.axis_size("grow")
    out_rows = half // columns
    grid = (nz, side, side)
    sems = 2 * supernodes * (4 if side > 1 else 1) * (4 * nz + 2) + supernodes * (1 + 2 * CHUNKS * (2 + nz))
    slot_total = block_lists.shape[1]
    slot_dev = slot_rows // BLK
    chosen_shape = (supernodes, own_rows, slot_total * BLK)
    smem = pl.BlockSpec(memory_space=pltpu.SMEM)
    chosen, live, hit = pl.pallas_call(
        functools.partial(choose, slot_dev),
        out_shape=(
            jax.ShapeDtypeStruct(chosen_shape, BF16),
            jax.ShapeDtypeStruct((supernodes, slot_dev), F32),
            jax.ShapeDtypeStruct((supernodes, own_rows // BLK, slot_total), F32),
        ),
        grid=(own_rows // step_rows,),
        in_specs=[smem, smem, pl.BlockSpec((step_rows, pool_width), lambda i: (i, 0))],
        out_specs=(
            pl.BlockSpec((supernodes, step_rows, slot_total * BLK), lambda i: (0, i, 0)),
            smem,
            smem,
        ),
        compiler_params=pltpu.CompilerParams(vmem_limit_bytes=58 * 1024 * 1024),
    )(live_counts, block_lists, ancestor_inverse)
    ancestor, diagonal = pl.pallas_call(
        functools.partial(kernel, sizes),
        out_shape=(
            jax.ShapeDtypeStruct((supernodes, own_rows, half), BF16),
            jax.ShapeDtypeStruct((supernodes, out_rows, order_size), F32),
        ),
        in_specs=[
            pl.BlockSpec(memory_space=pltpu.SMEM),
            pl.BlockSpec(memory_space=pltpu.SMEM),
            pl.BlockSpec(memory_space=pltpu.VMEM),
            pl.BlockSpec(memory_space=pltpu.VMEM),
            pl.BlockSpec(memory_space=pl.ANY),
        ],
        out_specs=(pl.BlockSpec(memory_space=pltpu.VMEM), pl.BlockSpec(memory_space=pltpu.VMEM)),
        scratch_shapes=[
            pltpu.VMEM(chosen_shape, BF16),
            pltpu.VMEM((supernodes,) + grid + (piece_rows, half), BF16),
            [pltpu.VMEM(grid + (slot_rows, half), BF16) for _ in range(supernodes)],
            pltpu.VMEM((supernodes, own_rows, half), F32),
            pltpu.VMEM((supernodes, own_rows // BLK, BLK, half), BF16),
            pltpu.VMEM((supernodes, own_rows, half), BF16),
            pltpu.VMEM((supernodes, own_rows, half), BF16),
            pltpu.VMEM((supernodes, 2) + grid + (out_rows, half), F32),
            pltpu.VMEM((supernodes, 2, CHUNKS, nz, out_rows, half // CHUNKS), F32),
            pltpu.VMEM((supernodes, 2, CHUNKS, nz, side, out_rows, half // CHUNKS), BF16),
            pltpu.VMEM((supernodes, 2, CHUNKS, nz, side, out_rows, half // CHUNKS), BF16),
            pltpu.VMEM((supernodes, 2, CHUNKS, nz, out_rows, half // CHUNKS), BF16),
            pltpu.VMEM((supernodes, 2, CHUNKS, nz, out_rows, half // CHUNKS), BF16),
            pltpu.VMEM((supernodes, 2, CHUNKS, nz, out_rows, half // CHUNKS), BF16),
            pltpu.VMEM((supernodes, 2, CHUNKS, nz, out_rows, half // CHUNKS), BF16),
            pltpu.SemaphoreType.DMA((sems,)),
            pltpu.SemaphoreType.DMA((sems,)),
            pltpu.SemaphoreType.DMA,
        ],
        compiler_params=pltpu.CompilerParams(
            collective_id=0, has_side_effects=True, vmem_limit_bytes=58 * 1024 * 1024
        ),
    )(live, hit, factor_inverse, lower_rows, chosen)
    return (ancestor, diagonal[:, None, :, :])


def solution(mesh):
    return jax.shard_map(
        shards,
        mesh=mesh,
        in_specs=(
            P(("groups", "gcol"), None),
            P("groups", "gcol", None),
            P("groups", "gcol", None),
            P("groups", None),
            P("groups"),
        ),
        out_specs=(P("groups", "gcol", "grow"), P("groups", "grow", "gcol", None)),
        check_vma=False,
    )
```
